32 devices in a mesh: groups: 2 (over y), seq: 4 (over z), mp: 2 (over x), rep: 2 (over core).
Axes of the slice: x: 2, y: 2, z: 4, core: 2. Of those that a mesh axis runs over, the one named last changes fastest.
Arguments:
- tokens: bfloat16 [8192, 2240], P(('groups', 'seq', 'rep')), parts along dimension 0, may hold values from -8 to 8
- slot_image: int32 [32], P(('groups', 'seq', 'rep')), parts along dimension 0, may hold values from 0 to 5, as said below
- modulation: float32 [12, 3, 2240], P('groups'), parts along dimension 0, may hold values from -3 to 3
- w_qkv: bfloat16 [2240, 3, 1280], P('rep', None, 'mp'), may hold values from -0.125 to 0.125
- w_out: bfloat16 [1280, 2240], P('rep', 'mp'), may hold values from -0.15625 to 0.15625
Outputs:
- updated: bfloat16 [8192, 2240], P(('groups', 'seq', 'rep'), 'mp'), parts along dimension 0
The draws below stay inside these ranges and needn't reach their ends.
There are 2 independent parts, one for each index of `groups`. The reference program is written for one: setup_inputs(seed, part) draws one part's arguments, and reference() takes and returns one part's arrays. A program takes and returns all parts, laid end to end along the dimension named above; an argument that names none is the same for every part. Nothing has to cross between parts.
Inputs may be any that keep to these rules, and one draw needn't show every extreme that they name: `slot_image`: every one of the 6 images owns one tile slot or more.
All inputs are finite; a program needn't handle non-finite values.
Results may differ from the reference program's by a relative error of at most 0.0036.
Values may be sent and summed in bfloat16 or wider, within the bound.
A program may use at most 128 MiB of HBM per device.

```python
import math
import jax
import jax.numpy as jnp
from jax import lax

D = 2240
HD = 32
HEADS = 40
TILE = 256
IMAGES = 6
SLOTS = 16
TOKENS = 4096


def slot_images(key):
    folded = jax.random.fold_in(key, 11)
    first, second = jax.random.split(folded)
    extra = jax.random.randint(first, (SLOTS - IMAGES,), 0, IMAGES).astype(jnp.int32)
    listed = jnp.concatenate([jnp.arange(IMAGES, dtype=jnp.int32), extra])
    return jax.random.permutation(second, listed).astype(jnp.int32)


def draw_slot_image(key, part):
    return slot_images(key)


def draw_tokens(key, part):
    owners = slot_images(key)
    folded = jax.random.fold_in(key, 23)
    key_mean, key_offset, key_scale, key_noise, key_factor, key_loading = jax.random.split(folded, 6)
    means = jax.random.normal(key_mean, (IMAGES, D), jnp.float32) * 0.7
    offsets = jax.random.normal(key_offset, (SLOTS, D), jnp.float32) * 0.5
    scales = jnp.exp(jax.random.uniform(key_scale, (SLOTS, 1, 1), jnp.float32, math.log(0.3), math.log(2.5)))
    factors = jax.random.normal(key_factor, (SLOTS, TILE, 8), jnp.float32)
    loadings = jax.random.normal(key_loading, (SLOTS, 8, D), jnp.float32) * 0.3
    noise = jax.random.normal(key_noise, (SLOTS, TILE, D), jnp.float32)
    latent = factors[:, :, 0:1] * loadings[:, 0:1, :]
    for index in range(1, 8):
        latent = latent + factors[:, :, index:index + 1] * loadings[:, index:index + 1, :]
    centers = means[owners] + offsets
    values = centers[:, None, :] + scales * (noise + latent)
    return jnp.clip(values, -8.0, 8.0).reshape(SLOTS * TILE, D).astype(jnp.bfloat16)


def block_scale(stream_key, shape, pieces, least, largest):
    gain, own = 1.0, jax.random.fold_in(stream_key, 6)
    for position, blocks in pieces:
        heights = jnp.exp(jax.random.uniform(jax.random.fold_in(own, position), (blocks,), jnp.float32, least / len(pieces), largest / len(pieces)))
        gain = gain * jnp.repeat(heights, shape[position] // blocks).reshape([-1 if axis == position else 1 for axis in range(len(shape))])
    return gain


def bell_draw(stream_key, extent, deviation, bound, cuts=(), held_as=jnp.bfloat16):
    gain = block_scale(stream_key, extent, cuts, -0.22, 0.18) if cuts else 1.0
    array = jax.random.normal(stream_key, extent, jnp.float32) * deviation * gain
    return jnp.minimum(jnp.maximum(array, -bound), bound).astype(held_as)


def setup_inputs(seed: int = 0, part: int = 0) -> dict:
    keys = jax.random.split(jax.random.key(seed), 6)
    own_keys = jax.random.split(jax.random.fold_in(keys[5], part), 6)
    tokens = draw_tokens(jax.random.fold_in(jax.random.fold_in(keys[5], part), 71), part)
    slot_image = draw_slot_image(jax.random.fold_in(jax.random.fold_in(keys[5], part), 71), part)
    modulation = bell_draw(own_keys[2], (IMAGES, 3, D), 1.0, 3.0, (), jnp.float32)
    w_qkv = bell_draw(keys[3], (D, 3, HEADS * HD), D ** -0.5, 0.125, ((0, 2), (2, 2)))
    w_out = bell_draw(keys[4], (HEADS * HD, D), (HEADS * HD) ** -0.5, 0.15625, ((0, 2), (1, 2)))
    return dict(tokens=tokens, slot_image=slot_image, modulation=modulation, w_qkv=w_qkv, w_out=w_out)


def reference(tokens, slot_image, modulation, w_qkv, w_out):
    hi = lax.Precision.HIGHEST
    picker = (slot_image[:, None] == jnp.arange(IMAGES, dtype=jnp.int32)[None, :]).astype(jnp.float32)
    per_tile = jnp.dot(picker, modulation.reshape(IMAGES, 3 * D), precision=hi).reshape(SLOTS, 3, D)
    xf = tokens.astype(jnp.float32).reshape(SLOTS, TILE, D)
    mean = lax.optimization_barrier(jnp.mean(xf, axis=2, keepdims=True))
    var = lax.optimization_barrier(jnp.mean((xf - mean) ** 2, axis=2, keepdims=True))
    normed = (xf - mean) / jnp.sqrt(var + 1e-06)
    modulated = (normed * (1.0 + per_tile[:, None, 1, :]) + per_tile[:, None, 0, :]).astype(jnp.bfloat16)
    qkv = jnp.dot(modulated.reshape(TOKENS, D), w_qkv.reshape(D, 3 * HEADS * HD), preferred_element_type=jnp.float32)
    qkv = qkv.reshape(SLOTS, TILE, 3, HEADS, HD)
    query = jax.nn.relu(qkv[:, :, 0]).astype(jnp.bfloat16).astype(jnp.float32)
    keyf = jax.nn.relu(qkv[:, :, 1]).astype(jnp.bfloat16).astype(jnp.float32)
    value = qkv[:, :, 2].astype(jnp.bfloat16).astype(jnp.float32)
    tile_state = jnp.einsum('slhe,slhf->shef', keyf, value, precision=hi)
    tile_ksum = lax.optimization_barrier(jnp.sum(keyf, axis=1))
    state = jnp.einsum('si,shef->ihef', picker, tile_state, precision=hi)
    ksum = jnp.einsum('si,she->ihe', picker, tile_ksum, precision=hi)
    own_state = jnp.einsum('si,ihef->shef', picker, state, precision=hi)
    own_ksum = jnp.einsum('si,ihe->she', picker, ksum, precision=hi)
    numer = jnp.einsum('slhe,shef->slhf', query, own_state, precision=hi)
    denom = jnp.einsum('slhe,she->slh', query, own_ksum, precision=hi) + 1e-06
    attn = (numer / denom[..., None]).astype(jnp.bfloat16).reshape(TOKENS, HEADS * HD)
    projected = jnp.dot(attn, w_out, preferred_element_type=jnp.float32).reshape(SLOTS, TILE, D)
    updated = xf + per_tile[:, None, 2, :] * projected
    return updated.astype(jnp.bfloat16).reshape(TOKENS, D)
```

```python
import functools

import jax
import jax.numpy as jnp
from jax import lax
from jax.experimental import pallas as pl
from jax.experimental.pallas import tpu as pltpu
from jax.sharding import PartitionSpec as P

D = 2240
HD = 32


def body(tokens, slot_image, modulation, w_qkv, w_out):
    hi = lax.Precision.HIGHEST
    tiles = slot_image.shape[0]
    rows = tokens.shape[0]
    tile_len = rows // tiles
    images = modulation.shape[0]
    width = w_qkv.shape[2]
    per_dev = width // HD
    picker = (slot_image[:, None] == jnp.arange(images, dtype=jnp.int32)[None, :]).astype(
        jnp.float32
    )
    per_tile = jnp.dot(picker, modulation.reshape(images, 3 * D), precision=hi).reshape(tiles, 3, D)
    xf = tokens.astype(jnp.float32).reshape(tiles, tile_len, D)
    mean = jnp.mean(xf, axis=2, keepdims=True)
    var = jnp.mean((xf - mean) ** 2, axis=2, keepdims=True)
    normed = (xf - mean) / jnp.sqrt(var + 1e-06)
    modulated = (normed * (1.0 + per_tile[:, None, 1, :]) + per_tile[:, None, 0, :]).astype(
        jnp.bfloat16
    )
    modulated = modulated.reshape(rows, D)
    qkv = jnp.einsum(
        "td,dcm->tcm",
        modulated,
        lax.all_gather(w_qkv, "rep", axis=0, tiled=True),
        preferred_element_type=jnp.float32,
    )
    qkv = qkv.reshape(tiles, tile_len, 3, per_dev, HD)
    query = jax.nn.relu(qkv[:, :, 0]).astype(jnp.bfloat16)
    keyf = jax.nn.relu(qkv[:, :, 1]).astype(jnp.bfloat16)
    value = qkv[:, :, 2].astype(jnp.bfloat16)
    tile_state = jnp.einsum("slhe,slhf->shef", keyf, value, preferred_element_type=jnp.float32)
    tile_ksum = jnp.sum(keyf.astype(jnp.float32), axis=1)
    state = jnp.einsum("si,shef->ihef", picker, tile_state, precision=hi)
    ksum = jnp.einsum("si,she->ihe", picker, tile_ksum, precision=hi)
    state, ksum = lax.psum((state, ksum), ("seq", "rep"))
    own_state = jnp.einsum("si,ihef->shef", picker, state, precision=hi)
    own_ksum = jnp.einsum("si,ihe->she", picker, ksum, precision=hi)
    query_wide = query.astype(jnp.float32)
    numer = jnp.einsum("slhe,shef->slhf", query_wide, own_state, precision=hi)
    denom = jnp.einsum("slhe,she->slh", query_wide, own_ksum, precision=hi) + 1e-06
    attn = (numer / denom[..., None]).astype(jnp.bfloat16).reshape(rows, per_dev * HD)
    out_full = lax.all_gather(w_out, "rep", axis=0, tiled=True)
    cols = out_full.shape[1]
    projected = jnp.dot(
        lax.all_gather(attn, "mp", axis=1, tiled=True), out_full, preferred_element_type=jnp.float32
    )
    offset = lax.axis_index("mp") * cols
    own_tokens = (
        lax.dynamic_slice_in_dim(tokens, offset, cols, 1)
        .astype(jnp.float32)
        .reshape(tiles, tile_len, cols)
    )
    gate = lax.dynamic_slice_in_dim(per_tile[:, 2, :], offset, cols, 1)
    updated = own_tokens + gate[:, None, :] * projected.reshape(tiles, tile_len, cols)
    return updated.astype(jnp.bfloat16).reshape(rows, cols)


MESH = pl.DeviceIdType.MESH
LANES = 128
NT = (((1,), (1,)), ((), ()))
TN = (((0,), (0,)), ((), ()))


def fused_kernel(
    nz, slot_ref, mod_ref, tok_hbm, w_hbm, wo_hbm, out_ref,
    tok, w, wo, modulated, q, k, v, att, gate, st, own,
    loc_sem, w_send, w_recv, q_send, q_recv, z_send, z_recv, f_send, f_recv, x_send, x_recv,
):
    f32, bf16 = jnp.float32, jnp.bfloat16
    z, m, r = lax.axis_index("seq"), lax.axis_index("mp"), lax.axis_index("rep")
    half, width = w_hbm.shape[1], w_hbm.shape[2]
    tiles = slot_ref.shape[0]
    tile_len = tok.shape[1] // tiles
    blocks = width // LANES
    out_rows = out_ref.shape[0]
    core, other_x = {"rep": 1 - r}, {"mp": 1 - m}

    def remote(src, dst, send, recv, device):
        return pltpu.make_async_remote_copy(
            src_ref=src, dst_ref=dst, send_sem=send, recv_sem=recv,
            device_id=device, device_id_type=MESH,
        )

    local = [pltpu.make_async_copy(tok_hbm, tok, loc_sem.at[0])]
    for c in range(3):
        local.append(pltpu.make_async_copy(w_hbm.at[c], w.at[r, c], loc_sem.at[1 + c]))
    local.append(pltpu.make_async_copy(wo_hbm, wo.at[r], loc_sem.at[4]))
    for copy in local:
        copy.start()

    barrier = pltpu.get_barrier_semaphore()
    pl.semaphore_signal(barrier, inc=1, device_id=core, device_id_type=MESH)
    pl.semaphore_signal(barrier, inc=1, device_id=other_x, device_id_type=MESH)
    for d in range(1, nz):
        pl.semaphore_signal(
            barrier, inc=1, device_id={"seq": lax.rem(z + d, nz)}, device_id_type=MESH
        )
    pl.semaphore_wait(barrier, nz + 1)

    weights = [remote(w_hbm.at[c], w.at[r, c], w_send.at[c], w_recv.at[c], core) for c in range(3)]
    weights.append(remote(wo_hbm, wo.at[r], w_send.at[3], w_recv.at[3], core))
    for copy in weights:
        copy.start()

    eye = (
        lax.broadcasted_iota(jnp.int32, (tile_len, tile_len), 0)
        == lax.broadcasted_iota(jnp.int32, (tile_len, tile_len), 1)
    ).astype(bf16)
    local[0].wait()
    for t in range(tiles):
        rows = slice(t * tile_len, (t + 1) * tile_len)
        table = mod_ref[slot_ref[t]]
        x = [
            lax.dot_general(
                eye, tok[h * half : (h + 1) * half, rows], NT, preferred_element_type=f32
            )
            for h in range(2)
        ]
        mean = (
            jnp.sum(x[0], axis=1, keepdims=True) + jnp.sum(x[1], axis=1, keepdims=True)
        ) / (2 * half)
        x = [y - mean for y in x]
        var = (
            jnp.sum(x[0] * x[0], axis=1, keepdims=True)
            + jnp.sum(x[1] * x[1], axis=1, keepdims=True)
        ) / (2 * half)
        scale = 1.0 / jnp.sqrt(var + 1e-06)
        for h in range(2):
            cols = slice(h * half, (h + 1) * half)
            modulated[h, rows, :] = (
                x[h] * scale * (1.0 + table[1:2, cols]) + table[0:1, cols]
            ).astype(bf16)

    def project(c, t):
        rows = slice(t * tile_len, (t + 1) * tile_len)
        return jnp.dot(modulated[0, rows, :], w[0, c], preferred_element_type=f32) + jnp.dot(
            modulated[1, rows, :], w[1, c], preferred_element_type=f32
        )

    queries = []
    for c in range(3):
        local[1 + c].wait()
        weights[c].wait()
        for t in range(tiles):
            rows = pl.ds(t * tile_len, tile_len)
            y = project(c, t)
            if c < 2:
                y = jnp.maximum(y, 0.0)
            y = y.astype(bf16)
            if c == 0:
                q[m, rows, :] = y
                copy = remote(
                    q.at[m, rows], q.at[m, rows], q_send.at[t], q_recv.at[t], other_x
                )
                copy.start()
                queries.append(copy)
            elif c == 1:
                k[rows, :] = y
            else:
                v[rows, :] = y

    row = lax.broadcasted_iota(jnp.int32, (LANES, LANES), 0)
    lane = lax.broadcasted_iota(jnp.int32, (LANES, LANES), 1)
    group = (lane // HD - row // HD + 4) % 4
    diagonal = group == 0
    inner = lane % HD
    zero = jnp.zeros((LANES, LANES), f32)
    ones = jnp.ones((tile_len, LANES), bf16)
    mine = 2 * z + r
    last = zero
    for t in range(tiles):
        rows = slice(t * tile_len, (t + 1) * tile_len)
        packed, sums = zero, zero
        for b in range(blocks):
            cols = slice(b * LANES, (b + 1) * LANES)
            both = lax.dot_general(
                k[rows, cols], jnp.concatenate([v[rows, cols], ones], axis=1), TN,
                preferred_element_type=f32,
            )
            s = jnp.where(diagonal, both[:, :LANES], 0.0)
            sums = jnp.where(jnp.logical_and(diagonal, inner == b), both[:, LANES:], sums)
            if b == 0:
                packed = s
            elif b < 4:
                packed = packed + pltpu.roll(s, HD * b, 1)
            else:
                last = last + (pltpu.roll(s, HD * t, 1) if t else s)
        last = last + pltpu.roll(sums, HD * (2 + t), 1)
        st[mine, t * LANES : (t + 1) * LANES, :] = packed.astype(bf16)
    st[mine, 2 * LANES : 3 * LANES, :] = last.astype(bf16)
    images = [jnp.full((8, LANES), slot_ref[t], jnp.int32).astype(f32) for t in range(tiles)]
    st[mine, 3 * LANES : 3 * LANES + 16, :] = jnp.concatenate(images, axis=0).astype(bf16)

    across = []
    for d in range(1, nz):
        across.append(
            remote(
                st.at[mine], st.at[mine], z_send.at[d], z_recv.at[d],
                {"seq": lax.rem(z + d, nz)},
            )
        )
        across[-1].start()
    forwards = [remote(st.at[mine], st.at[mine], f_send.at[0], f_recv.at[0], core)]
    forwards[0].start()

    for t in range(tiles):
        table = mod_ref[slot_ref[t]]
        for start in range(0, 2 * half, LANES):
            stop = min(start + LANES, 2 * half)
            gate[t, start:stop, :] = jnp.broadcast_to(
                table[2:3, start:stop], (LANES, stop - start)
            ).T

    for d in range(1, nz):
        across[d - 1].wait_recv()
        source = 2 * lax.rem(z - d + nz, nz) + r
        forwards.append(
            remote(st.at[source], st.at[source], f_send.at[d], f_recv.at[d], core)
        )
        forwards[d].start()
    for copy in forwards:
        copy.wait_recv()

    even = group % 2 == 0
    pair = zero
    for t in range(tiles):
        target = images[t][0:1]

        def gather(i, carry, target=target):
            a, c = carry
            ids = st[i, 3 * LANES : 3 * LANES + 16, :].astype(f32)
            first = jnp.where(ids[0:1] == target, 1.0, 0.0)
            second = jnp.where(ids[8:9] == target, 1.0, 0.0)
            a = a + first * st[i, 0:LANES, :].astype(f32)
            a = a + second * st[i, LANES : 2 * LANES, :].astype(f32)
            c = c + jnp.where(even, first, second) * st[i, 2 * LANES : 3 * LANES, :].astype(f32)
            return a, c

        a, c = lax.fori_loop(0, 2 * nz, gather, (zero, zero))
        own[m, t * LANES : (t + 1) * LANES, :] = a.astype(bf16)
        c = jnp.where(even, c + pltpu.roll(c, LANES - HD, 1), 0.0)
        pair = pair + (pltpu.roll(c, HD * t, 1) if t else c)
    own[m, 2 * LANES : 3 * LANES, :] = pair.astype(bf16)
    states = remote(own.at[m], own.at[m], x_send.at[0], x_recv.at[0], other_x)
    states.start()

    def attend(j):
        rest = own[j, 2 * LANES : 3 * LANES, :].astype(f32)
        for t in range(tiles):
            rows = slice(t * tile_len, (t + 1) * tile_len)
            packed = own[j, t * LANES : (t + 1) * LANES, :].astype(f32)
            sums = jnp.where(diagonal, pltpu.roll(rest, LANES - HD * (2 + t), 1), 0.0)
            for b in range(blocks):
                cols = slice(b * LANES, (b + 1) * LANES)
                if b < 4:
                    s = pltpu.roll(packed, LANES - HD * b, 1) if b else packed
                else:
                    s = pltpu.roll(rest, LANES - HD * t, 1) if t else rest
                s = jnp.where(diagonal, s, 0.0)
                ksum = jnp.sum(jnp.where(inner == b, sums, 0.0), axis=1, keepdims=True)
                ksum = jnp.where(diagonal, ksum, 0.0)
                both = jnp.dot(
                    q[j, rows, cols], jnp.concatenate([s, ksum], axis=1).astype(bf16),
                    preferred_element_type=f32,
                )
                att[j, rows, cols] = (both[:, :LANES] / (both[:, LANES:] + 1e-06)).astype(bf16)

    attend(m)
    local[4].wait()
    weights[3].wait()
    for copy in queries:
        copy.wait()
    states.wait()
    attend(1 - m)

    step = out_rows // 2
    for t in range(tiles):
        rows = slice(t * tile_len, (t + 1) * tile_len)
        for start in range(0, out_rows, step):
            part = pl.ds(pl.multiple_of(m * out_rows + start, 16), step)
            projected = lax.dot_general(
                wo[0, start : start + step, :], att[0, rows, :], NT, preferred_element_type=f32
            ) + lax.dot_general(
                wo[1, start : start + step, :], att[1, rows, :], NT, preferred_element_type=f32
            )
            g = gate[t, part, :]
            g = jnp.concatenate([g] * (tile_len // LANES), axis=1)
            out_ref[start : start + step, rows] = (
                tok[part, rows].astype(f32) + g * projected
            ).astype(bf16)
    for copy in across + forwards:
        copy.wait_send()


def fused(nz, tokens, slot_image, modulation, w_qkv, w_out):
    rows, d = tokens.shape
    half, _, width = w_qkv.shape
    cols = w_out.shape[1]
    tiles = slot_image.shape[0]
    bf16 = jnp.bfloat16
    any_spec = pl.BlockSpec(memory_space=pl.ANY)
    dma = pltpu.SemaphoreType.DMA
    out = pl.pallas_call(
        functools.partial(fused_kernel, nz),
        out_shape=jax.ShapeDtypeStruct((cols, rows), bf16),
        in_specs=[
            pl.BlockSpec(memory_space=pltpu.SMEM),
            pl.BlockSpec(memory_space=pltpu.VMEM),
            any_spec,
            any_spec,
            any_spec,
        ],
        out_specs=pl.BlockSpec(memory_space=pltpu.VMEM),
        scratch_shapes=[
            pltpu.VMEM((d, rows), bf16),
            pltpu.VMEM((2, 3, half, width), bf16),
            pltpu.VMEM((2, cols, width), bf16),
            pltpu.VMEM((2, rows, half), bf16),
            pltpu.VMEM((2, rows, width), bf16),
            pltpu.VMEM((rows, width), bf16),
            pltpu.VMEM((rows, width), bf16),
            pltpu.VMEM((2, rows, width), bf16),
            pltpu.VMEM((tiles, d, LANES), jnp.float32),
            pltpu.VMEM((2 * nz, 3 * LANES + 16, LANES), bf16),
            pltpu.VMEM((2, 3 * LANES, LANES), bf16),
            dma((5,)), dma((4,)), dma((4,)), dma((tiles,)), dma((tiles,)),
            dma((nz,)), dma((nz,)), dma((nz,)), dma((nz,)), dma((1,)), dma((1,)),
        ],
        compiler_params=pltpu.CompilerParams(
            collective_id=0, has_side_effects=True, vmem_limit_bytes=56 * 1024 * 1024
        ),
    )(slot_image, modulation, tokens.T, jnp.transpose(w_qkv, (1, 0, 2)), w_out.T)
    return out.T


def choose(nz, mp, reps, tokens, slot_image, modulation, w_qkv, w_out):
    rows, d = tokens.shape
    half, _, width = w_qkv.shape
    tiles = slot_image.shape[0]
    fits = (
        mp == 2 and reps == 2 and tiles == 2 and width == 5 * LANES
        and w_out.shape[0] == width and LANES % HD == 0 and modulation.shape[0] <= 256
        and (rows // tiles) % LANES == 0 and half % 16 == 0 and w_out.shape[1] % 32 == 0
    )
    if fits:
        return fused(nz, tokens, slot_image, modulation, w_qkv, w_out)
    return body(tokens, slot_image, modulation, w_qkv, w_out)


def solution(mesh):
    return jax.shard_map(
        functools.partial(choose, mesh.shape["seq"], mesh.shape["mp"], mesh.shape["rep"]),
        mesh=mesh,
        in_specs=(
            P(("groups", "seq", "rep"), None),
            P(("groups", "seq", "rep")),
            P("groups", None, None),
            P("rep", None, "mp"),
            P("rep", "mp"),
        ),
        out_specs=P(("groups", "seq", "rep"), "mp"),
        check_vma=False,
    )
```

```python
import functools

import jax
import jax.numpy as jnp
from jax import lax
from jax.experimental import pallas as pl
from jax.experimental.pallas import tpu as pltpu
from jax.sharding import PartitionSpec as P

D = 2240
HD = 32


def body(tokens, slot_image, modulation, w_qkv, w_out):
    hi = lax.Precision.HIGHEST
    tiles = slot_image.shape[0]
    rows = tokens.shape[0]
    tile_len = rows // tiles
    images = modulation.shape[0]
    width = w_qkv.shape[2]
    per_dev = width // HD
    picker = (slot_image[:, None] == jnp.arange(images, dtype=jnp.int32)[None, :]).astype(
        jnp.float32
    )
    per_tile = jnp.dot(picker, modulation.reshape(images, 3 * D), precision=hi).reshape(tiles, 3, D)
    xf = tokens.astype(jnp.float32).reshape(tiles, tile_len, D)
    mean = jnp.mean(xf, axis=2, keepdims=True)
    var = jnp.mean((xf - mean) ** 2, axis=2, keepdims=True)
    normed = (xf - mean) / jnp.sqrt(var + 1e-06)
    modulated = (normed * (1.0 + per_tile[:, None, 1, :]) + per_tile[:, None, 0, :]).astype(
        jnp.bfloat16
    )
    modulated = modulated.reshape(rows, D)
    qkv = jnp.einsum(
        "td,dcm->tcm",
        modulated,
        lax.all_gather(w_qkv, "rep", axis=0, tiled=True),
        preferred_element_type=jnp.float32,
    )
    qkv = qkv.reshape(tiles, tile_len, 3, per_dev, HD)
    query = jax.nn.relu(qkv[:, :, 0]).astype(jnp.bfloat16)
    keyf = jax.nn.relu(qkv[:, :, 1]).astype(jnp.bfloat16)
    value = qkv[:, :, 2].astype(jnp.bfloat16)
    tile_state = jnp.einsum("slhe,slhf->shef", keyf, value, preferred_element_type=jnp.float32)
    tile_ksum = jnp.sum(keyf.astype(jnp.float32), axis=1)
    state = jnp.einsum("si,shef->ihef", picker, tile_state, precision=hi)
    ksum = jnp.einsum("si,she->ihe", picker, tile_ksum, precision=hi)
    state, ksum = lax.psum((state, ksum), ("seq", "rep"))
    own_state = jnp.einsum("si,ihef->shef", picker, state, precision=hi)
    own_ksum = jnp.einsum("si,ihe->she", picker, ksum, precision=hi)
    query_wide = query.astype(jnp.float32)
    numer = jnp.einsum("slhe,shef->slhf", query_wide, own_state, precision=hi)
    denom = jnp.einsum("slhe,she->slh", query_wide, own_ksum, precision=hi) + 1e-06
    attn = (numer / denom[..., None]).astype(jnp.bfloat16).reshape(rows, per_dev * HD)
    out_full = lax.all_gather(w_out, "rep", axis=0, tiled=True)
    cols = out_full.shape[1]
    projected = jnp.dot(
        lax.all_gather(attn, "mp", axis=1, tiled=True), out_full, preferred_element_type=jnp.float32
    )
    offset = lax.axis_index("mp") * cols
    own_tokens = (
        lax.dynamic_slice_in_dim(tokens, offset, cols, 1)
        .astype(jnp.float32)
        .reshape(tiles, tile_len, cols)
    )
    gate = lax.dynamic_slice_in_dim(per_tile[:, 2, :], offset, cols, 1)
    updated = own_tokens + gate[:, None, :] * projected.reshape(tiles, tile_len, cols)
    return updated.astype(jnp.bfloat16).reshape(rows, cols)


MESH = pl.DeviceIdType.MESH
LANES = 128
NT = (((1,), (1,)), ((), ()))
TN = (((0,), (0,)), ((), ()))


def fused_kernel(
    nz, slot_ref, mod_ref, tok_hbm, w_hbm, wo_hbm, out_ref,
    tok, w, wo, modulated, q, k, v, att, gate, snd, st, res, own, acc,
    loc_sem, w_send, w_recv, q_send, q_recv, z_send, z_recv, x_send, x_recv,
):
    f32, bf16 = jnp.float32, jnp.bfloat16
    z, m, r = lax.axis_index("seq"), lax.axis_index("mp"), lax.axis_index("rep")
    half, width = w_hbm.shape[1], w_hbm.shape[2]
    tiles = slot_ref.shape[0]
    tile_len = tok.shape[1] // tiles
    blocks = width // LANES
    out_rows = out_ref.shape[0]
    core, other_x = {"rep": 1 - r}, {"mp": 1 - m}

    def remote(src, dst, send, recv, device):
        return pltpu.make_async_remote_copy(
            src_ref=src, dst_ref=dst, send_sem=send, recv_sem=recv,
            device_id=device, device_id_type=MESH,
        )

    local = [pltpu.make_async_copy(tok_hbm, tok, loc_sem.at[0])]
    for c in range(3):
        local.append(pltpu.make_async_copy(w_hbm.at[c], w.at[r, c], loc_sem.at[1 + c]))
    local.append(pltpu.make_async_copy(wo_hbm, wo.at[r], loc_sem.at[4]))
    for copy in local:
        copy.start()

    parts = 2 * nz
    part = LANES // parts
    mine = 2 * z + r

    def member(d, e):
        p = lax.rem(mine + d, parts)
        return {"seq": p // 2, "rep": lax.rem(p, 2), "mp": lax.rem(m + e, 2)}

    barrier = pltpu.get_barrier_semaphore()
    for e in range(2):
        for d in range(parts):
            if d or e:
                pl.semaphore_signal(
                    barrier, inc=1, device_id=member(d, e), device_id_type=MESH
                )
    pl.semaphore_wait(barrier, 2 * parts - 1)

    weights = [remote(w_hbm.at[c], w.at[r, c], w_send.at[c], w_recv.at[c], core) for c in range(3)]
    weights.append(remote(wo_hbm, wo.at[r], w_send.at[3], w_recv.at[3], core))
    weights[0].start()

    eye = (
        lax.broadcasted_iota(jnp.int32, (tile_len, tile_len), 0)
        == lax.broadcasted_iota(jnp.int32, (tile_len, tile_len), 1)
    ).astype(bf16)
    local[0].wait()
    def normalize(t):
        rows = slice(t * tile_len, (t + 1) * tile_len)
        table = mod_ref[slot_ref[t]]
        x = [
            lax.dot_general(
                eye, tok[h * half : (h + 1) * half, rows], NT, preferred_element_type=f32
            )
            for h in range(2)
        ]
        mean = (
            jnp.sum(x[0], axis=1, keepdims=True) + jnp.sum(x[1], axis=1, keepdims=True)
        ) / (2 * half)
        x = [y - mean for y in x]
        var = (
            jnp.sum(x[0] * x[0], axis=1, keepdims=True)
            + jnp.sum(x[1] * x[1], axis=1, keepdims=True)
        ) / (2 * half)
        scale = 1.0 / jnp.sqrt(var + 1e-06)
        for h in range(2):
            cols = slice(h * half, (h + 1) * half)
            modulated[h, rows, :] = (
                x[h] * scale * (1.0 + table[1:2, cols]) + table[0:1, cols]
            ).astype(bf16)

    def project(c, t):
        rows = slice(t * tile_len, (t + 1) * tile_len)
        return jnp.dot(modulated[0, rows, :], w[0, c], preferred_element_type=f32) + jnp.dot(
            modulated[1, rows, :], w[1, c], preferred_element_type=f32
        )

    local[1].wait()
    queries = []
    for t in range(tiles):
        rows = pl.ds(t * tile_len, tile_len)
        normalize(t)
        if t == 0:
            weights[0].wait()
            weights[1].start()
            weights[2].start()
        q[m, rows, :] = jnp.maximum(project(0, t), 0.0).astype(bf16)
        queries.append(remote(q.at[m, rows], q.at[m, rows], q_send.at[t], q_recv.at[t], other_x))
        queries[t].start()
    for c, dest in ((1, k), (2, v)):
        local[1 + c].wait()
        weights[c].wait()
        if c == 1:
            weights[3].start()
        for t in range(tiles):
            y = project(c, t)
            if c == 1:
                y = jnp.maximum(y, 0.0)
            dest[t * tile_len : (t + 1) * tile_len, :] = y.astype(bf16)

    row = lax.broadcasted_iota(jnp.int32, (LANES, LANES), 0)
    lane = lax.broadcasted_iota(jnp.int32, (LANES, LANES), 1)
    group = (lane // HD - row // HD + 4) % 4
    diagonal = group == 0
    inner = lane % HD
    zero = jnp.zeros((LANES, LANES), f32)
    ones = jnp.ones((tile_len, LANES), bf16)
    last = zero
    outgoing = []
    for t in range(tiles):
        rows = slice(t * tile_len, (t + 1) * tile_len)
        packed, sums = zero, zero
        for b in range(blocks):
            cols = slice(b * LANES, (b + 1) * LANES)
            both = lax.dot_general(
                k[rows, cols], jnp.concatenate([v[rows, cols], ones], axis=1), TN,
                preferred_element_type=f32,
            )
            s = jnp.where(diagonal, both[:, :LANES], 0.0)
            sums = jnp.where(jnp.logical_and(diagonal, inner == b), both[:, LANES:], sums)
            if b == 0:
                packed = s
            elif b < 4:
                packed = packed + pltpu.roll(s, HD * b, 1)
            else:
                last = last + (pltpu.roll(s, HD * t, 1) if t else s)
        last = last + pltpu.roll(sums, HD * (2 + t), 1)
        outgoing.append(packed.astype(bf16))
    outgoing.append(last.astype(bf16))
    images = [jnp.full((8, LANES), slot_ref[t], jnp.int32).astype(f32) for t in range(tiles)]
    images = jnp.concatenate(images, axis=0).astype(bf16)
    for i in range(parts):
        for n in range(3):
            snd[i, n * part : (n + 1) * part, :] = outgoing[n][i * part : (i + 1) * part]
        snd[i, 3 * part : 3 * part + 16, :] = images
    scatter = []
    for d in range(1, parts):
        p = lax.rem(mine + d, parts)
        scatter.append(
            remote(snd.at[p], st.at[mine], z_send.at[d], z_recv.at[d], member(d, 0))
        )
        scatter[-1].start()
    st[mine] = snd[mine]

    for t in range(tiles):
        table = mod_ref[slot_ref[t]]
        for start in range(0, 2 * half, LANES):
            stop = min(start + LANES, 2 * half)
            gate[t, start:stop, :] = jnp.broadcast_to(
                table[2:3, start:stop], (LANES, stop - start)
            ).T

    for copy in scatter:
        copy.wait()

    small_row = lax.broadcasted_iota(jnp.int32, (part, LANES), 0) + mine * part
    small_lane = lax.broadcasted_iota(jnp.int32, (part, LANES), 1)
    even = (small_lane // HD + small_row // HD) % 2 == 0

    @pl.loop(0, parts)
    def reduce(d):
        p = lax.rem(mine + d, parts)
        pair = None
        for t in range(tiles):
            target = st[p, 3 * part : 3 * part + 16, :].astype(f32)[8 * t : 8 * t + 1]
            a = jnp.zeros((part, LANES), f32)
            c = jnp.zeros((part, LANES), f32)
            for i in range(parts):
                block = st[i].astype(f32)
                first = jnp.where(block[3 * part : 3 * part + 1] == target, 1.0, 0.0)
                second = jnp.where(block[3 * part + 8 : 3 * part + 9] == target, 1.0, 0.0)
                a = a + first * block[:part] + second * block[part : 2 * part]
                c = c + jnp.where(even, first, second) * block[2 * part : 3 * part]
            res[p, t * part : (t + 1) * part, :] = a.astype(bf16)
            c = jnp.where(even, c + pltpu.roll(c, LANES - HD, 1), 0.0)
            pair = pair + pltpu.roll(c, HD * t, 1) if t else c
        res[p, 2 * part : 3 * part, :] = pair.astype(bf16)

        @pl.when(d > 0)
        def _():
            remote(
                res.at[p], own.at[m, mine], x_send.at[d], x_recv.at[d], member(d, 0)
            ).start()

    states = [[], []]
    for e in range(2):
        for d in range(parts):
            if d or e:
                p = lax.rem(mine + d, parts)
                copy = remote(
                    res.at[p], own.at[m, mine], x_send.at[parts * e + d],
                    x_recv.at[parts * e + d], member(d, e),
                )
                if e:
                    copy.start()
                states[e].append(copy)
    own[m, mine] = res[mine]

    def attend(j):
        rest = own[j, :, 2 * part : 3 * part, :].astype(f32).reshape(LANES, LANES)
        for t in range(tiles):
            rows = slice(t * tile_len, (t + 1) * tile_len)
            packed = own[j, :, t * part : (t + 1) * part, :].astype(f32).reshape(LANES, LANES)
            sums = jnp.where(diagonal, pltpu.roll(rest, LANES - HD * (2 + t), 1), 0.0)
            for b in range(blocks):
                cols = slice(b * LANES, (b + 1) * LANES)
                if b < 4:
                    s = pltpu.roll(packed, LANES - HD * b, 1) if b else packed
                else:
                    s = pltpu.roll(rest, LANES - HD * t, 1) if t else rest
                s = jnp.where(diagonal, s, 0.0)
                ksum = jnp.sum(jnp.where(inner == b, sums, 0.0), axis=1, keepdims=True)
                ksum = jnp.where(diagonal, ksum, 0.0)
                both = jnp.dot(
                    q[j, rows, cols], jnp.concatenate([s, ksum], axis=1).astype(bf16),
                    preferred_element_type=f32,
                )
                att[j, rows, cols] = (both[:, :LANES] / (both[:, LANES:] + 1e-06)).astype(bf16)

    step = out_rows // 2

    def output(j, finish):
        for t in range(tiles):
            rows = slice(t * tile_len, (t + 1) * tile_len)
            for start in range(0, out_rows, step):
                here = slice(start, start + step)
                part = pl.ds(pl.multiple_of(m * out_rows + start, 16), step)
                projected = lax.dot_general(
                    wo[j, here, :], att[j, rows, :], NT, preferred_element_type=f32
                )
                g = gate[t, part, :]
                g = jnp.concatenate([g] * (tile_len // LANES), axis=1)
                if finish:
                    out_ref[here, rows] = (acc[here, rows] + g * projected).astype(bf16)
                else:
                    acc[here, rows] = tok[part, rows].astype(f32) + g * projected

    for copy in states[0]:
        copy.wait()
    attend(m)
    local[4].wait()
    weights[3].wait()
    output(m, False)
    for copy in queries:
        copy.wait()
    for copy in states[1]:
        copy.wait()
    attend(1 - m)
    output(1 - m, True)


def fused(nz, tokens, slot_image, modulation, w_qkv, w_out):
    rows, d = tokens.shape
    half, _, width = w_qkv.shape
    cols = w_out.shape[1]
    tiles = slot_image.shape[0]
    parts = 2 * nz
    part = LANES // parts
    bf16 = jnp.bfloat16
    any_spec = pl.BlockSpec(memory_space=pl.ANY)
    dma = pltpu.SemaphoreType.DMA
    out = pl.pallas_call(
        functools.partial(fused_kernel, nz),
        out_shape=jax.ShapeDtypeStruct((cols, rows), bf16),
        in_specs=[
            pl.BlockSpec(memory_space=pltpu.SMEM),
            pl.BlockSpec(memory_space=pltpu.VMEM),
            any_spec,
            any_spec,
            any_spec,
        ],
        out_specs=pl.BlockSpec(memory_space=pltpu.VMEM),
        scratch_shapes=[
            pltpu.VMEM((d, rows), bf16),
            pltpu.VMEM((2, 3, half, width), bf16),
            pltpu.VMEM((2, cols, width), bf16),
            pltpu.VMEM((2, rows, half), bf16),
            pltpu.VMEM((2, rows, width), bf16),
            pltpu.VMEM((rows, width), bf16),
            pltpu.VMEM((rows, width), bf16),
            pltpu.VMEM((2, rows, width), bf16),
            pltpu.VMEM((tiles, d, LANES), jnp.float32),
            pltpu.VMEM((parts, 3 * part + 16, LANES), bf16),
            pltpu.VMEM((parts, 3 * part + 16, LANES), bf16),
            pltpu.VMEM((parts, 3 * part, LANES), bf16),
            pltpu.VMEM((2, parts, 3 * part, LANES), bf16),
            pltpu.VMEM((cols, rows), jnp.float32),
            dma((5,)), dma((4,)), dma((4,)), dma((tiles,)), dma((tiles,)),
            dma((parts,)), dma((parts,)), dma((2 * parts,)), dma((2 * parts,)),
        ],
        compiler_params=pltpu.CompilerParams(
            collective_id=0, has_side_effects=True, vmem_limit_bytes=56 * 1024 * 1024
        ),
    )(slot_image, modulation, tokens.T, jnp.transpose(w_qkv, (1, 0, 2)), w_out.T)
    return out.T


def choose(nz, mp, reps, tokens, slot_image, modulation, w_qkv, w_out):
    rows, d = tokens.shape
    half, _, width = w_qkv.shape
    tiles = slot_image.shape[0]
    fits = (
        nz in (1, 2, 4) and mp == 2 and reps == 2 and tiles == 2 and width == 5 * LANES
        and w_out.shape[0] == width and LANES % HD == 0 and modulation.shape[0] <= 256
        and (rows // tiles) % LANES == 0 and half % 16 == 0 and w_out.shape[1] % 32 == 0
    )
    if fits:
        return fused(nz, tokens, slot_image, modulation, w_qkv, w_out)
    return body(tokens, slot_image, modulation, w_qkv, w_out)


def solution(mesh):
    return jax.shard_map(
        functools.partial(choose, mesh.shape["seq"], mesh.shape["mp"], mesh.shape["rep"]),
        mesh=mesh,
        in_specs=(
            P(("groups", "seq", "rep"), None),
            P(("groups", "seq", "rep")),
            P("groups", None, None),
            P("rep", None, "mp"),
            P("rep", "mp"),
        ),
        out_specs=P(("groups", "seq", "rep"), "mp"),
        check_vma=False,
    )
```
